256 devices in a mesh: pipe: 8 (over y, x_lo), expert: 32 (over z, x_hi, core).
Axes of the slice: x: 4 (x_hi: 2, x_lo: 2; x = x_hi * 2 + x_lo), y: 4, z: 8, core: 2. Of those that a mesh axis runs over, the one named last changes fastest.
Arguments:
- fwd_prev: bfloat16 [8, 4096, 3584], P('pipe', 'expert'), may hold values from -6 to 6
- bwd_next: bfloat16 [8, 4096, 3584], P('pipe', 'expert'), may hold values from -6 to 6
- bwd_input: bfloat16 [8, 4096, 3584], P('pipe', 'expert'), may hold values from -6 to 6
- norm_gain: float32 [8, 3584], P('pipe'), may hold values from 0.1 to 1.9
- w_gate: bfloat16 [8, 3584, 8192], P('pipe', None, 'expert'), may hold values from -0.09375 to 0.09375
- w_up: bfloat16 [8, 3584, 8192], P('pipe', None, 'expert'), may hold values from -0.09375 to 0.09375
- w_down: bfloat16 [8, 8192, 3584], P('pipe', 'expert'), may hold values from -0.375 to 0.375
- fwd_routes: int32 [8, 4096, 1], P('pipe', 'expert'), may hold values from 0 to 7; in each aligned block of 128 rows (0 to 127, 128 to 255, ..., all dimensions but the last counted through in order) at most 24 rows name the same one
- fwd_gates: float32 [8, 4096, 1], P('pipe', 'expert'), may hold values from 0.2 to 1
- bwd_routes: int32 [8, 4096, 1], P('pipe', 'expert'), may hold values from 0 to 7; in each aligned block of 128 rows (0 to 127, 128 to 255, ..., all dimensions but the last counted through in order) at most 24 rows name the same one
- bwd_gates: float32 [8, 4096, 1], P('pipe', 'expert'), may hold values from 0.2 to 1
Outputs:
- fwd_out: bfloat16 [8, 4096, 3584], P('pipe', 'expert')
- bwd_grad: bfloat16 [8, 4096, 3584], P('pipe', 'expert')
- gain_grad: float32 [8, 3584], P('pipe')
The draws below stay inside these ranges and needn't reach their ends.
Inputs may be any that keep to these rules, and one draw needn't show every extreme that they name: `fwd_routes`: within each device's 128 tokens (one aligned block of rows), a token's 1 picks are different experts and no expert is picked more than 24 times. `bwd_routes`: within each device's 128 tokens (one aligned block of rows), a token's 1 picks are different experts and no expert is picked more than 24 times.
All inputs are finite; a program needn't handle non-finite values.
Results may differ from the reference program's by a relative error of at most 0.0067.
Values may be sent and summed in bfloat16 or wider, within the bound.
A program may use at most 128 MiB of HBM per device.

```python
import math
import jax
import jax.numpy as jnp
import numpy as np
from jax import lax

D = 3584
HID_W = 1024
EXPERTS = 8
TOP = 1
TOK_DEV = 128
CAP = 24
SPLIT = 4
SLICE = 256
TOKENS = 4096
SECTIONS = 8
N_EXPERT = 32


def block_scale(rng, shape, cuts, least, high):
    level = 1.0
    for dim, parts in cuts:
        steps = jax.random.uniform(jax.random.fold_in(jax.random.fold_in(rng, 6), dim), (parts,), jnp.float32, least / len(cuts), high / len(cuts))
        level = level * jnp.repeat(jnp.exp(steps), shape[dim] // parts).reshape((-1,) + (1,) * (len(shape) - 1 - dim))
    return level


def shared_out(key, own, number, rows, number_of, top, most, lean):
    order = jax.random.permutation(key, number_of)
    crowded, ordinary = shares(number_of, rows * top, most, lean, True), shares(number_of, rows * top, most, lean, False)
    places = jnp.arange(number_of)

    def named(tallies, turn):
        used = int((tallies > 0).sum())
        fixed = max(1, used // 4)
        shifted = fixed + (places - fixed + turn * (used - fixed)) % max(1, number_of - fixed)
        return jnp.zeros((number_of,), jnp.int32).at[order[jnp.where(places < fixed, places, shifted)]].set(jnp.asarray(tallies, jnp.int32))

    tallies = jnp.where(number % 4 == 0, named(crowded, number // 4), named(ordinary, number - number // 4 - 1))
    mixed = jax.random.permutation(jax.random.fold_in(own, 3), number_of)
    giver, sink = mixed[0:number_of // 2 * 2:2], mixed[1:number_of // 2 * 2:2]
    room = jnp.minimum(tallies[giver] - 1, most - tallies[sink]) // 2
    room = jnp.where((giver == order[0]) | (sink == order[0]) | (tallies[sink] == 0), 0, jnp.maximum(room, 0))
    shifted = jax.random.randint(jax.random.fold_in(own, 4), (number_of // 2,), 0, 1 << 20) % (room + 1)
    tallies = tallies.at[giver].add(-shifted).at[sink].add(shifted)
    labels = jnp.searchsorted(jnp.cumsum(tallies), jnp.arange(rows * top), side="right").astype(jnp.int32)
    table = labels.reshape(top, rows).T
    table = table[jax.random.permutation(jax.random.fold_in(own, 1), rows)]
    turn = jax.random.randint(jax.random.fold_in(own, 2), (rows, 1), 0, top)
    return jnp.take_along_axis(table, (jnp.arange(top)[None, :] + turn) % top, axis=1)


def shares(number_of, total, reach, slope, full):
    loads = [(1 << 20) // math.isqrt(grade ** slope) + 1 for grade in range(1, number_of + 1)]
    largest = reach if full else min(reach, max(-(-total // number_of), total * loads[0] // sum(loads)))
    least = 1 if total - largest >= number_of - 1 else 0
    holding, surplus = [largest] + [least] * (number_of - 1), total - largest - least * (number_of - 1)
    while surplus > 0:
        free = [i for i in range(1, number_of) if holding[i] < largest] or [i for i in range(1, number_of) if holding[i] < reach]
        mass, remaining = sum([loads[i] for i in free]), surplus
        for i in free:
            addition = min(reach - holding[i], max(1, remaining * loads[i] // mass), surplus)
            holding[i] = holding[i] + addition
            surplus = surplus - addition
    return np.array(holding)


def bell_draw(stream_key, dims, deviation, reach, split=(), kind=jnp.bfloat16):
    gain = block_scale(stream_key, dims, split, -0.22, 0.18) if split else 1.0
    array = jax.random.normal(stream_key, dims, jnp.float32) * deviation * gain
    return jnp.minimum(jnp.maximum(array, -reach), reach).astype(kind)


def setup_inputs(seed: int = 0) -> dict:
    seeds = jax.random.split(jax.random.key(seed), 12)
    fwd_prev = bell_draw(seeds[0], (SECTIONS, TOKENS, D), 1.0, 6.0, ((0, 8), (1, 32)))
    bwd_next = bell_draw(seeds[1], (SECTIONS, TOKENS, D), 1.0, 6.0, ((0, 8), (1, 32)))
    bwd_input = bell_draw(seeds[2], (SECTIONS, TOKENS, D), 1.0, 6.0, ((0, 8), (1, 32)))
    norm_gain = jnp.clip(1.0 + 0.18 * jax.random.normal(seeds[3], (SECTIONS, D), jnp.float32), 0.1, 1.9)
    w_gate = bell_draw(seeds[4], (SECTIONS, D, EXPERTS * HID_W), D ** -0.5, 0.09375, ((0, 8), (2, 32)))
    w_up = bell_draw(seeds[5], (SECTIONS, D, EXPERTS * HID_W), D ** -0.5, 0.09375, ((0, 8), (2, 32)))
    w_down = bell_draw(seeds[6], (SECTIONS, EXPERTS * HID_W, D), (HID_W // 4) ** -0.5, 0.375, ((0, 8), (1, 32)))
    fwd_routes_keys = jax.random.split(jax.random.fold_in(seeds[7], 1), SECTIONS * TOKENS // TOK_DEV)
    fwd_routes_turns = jax.random.permutation(jax.random.fold_in(seeds[7], 3), SECTIONS * TOKENS // TOK_DEV)
    fwd_routes = jax.vmap(lambda own, number: shared_out(jax.random.fold_in(seeds[7], 2), own, number, TOK_DEV, EXPERTS, TOP, CAP, 2))(fwd_routes_keys, fwd_routes_turns).reshape((SECTIONS, TOKENS, TOP))
    fwd_gates = jnp.clip(0.2 + 0.8 * jax.random.uniform(seeds[8], (SECTIONS, TOKENS, TOP), jnp.float32) ** block_scale(seeds[8], (SECTIONS, TOKENS, TOP), ((0, 8), (1, 32)), -0.2, 0.2), 0.2, 1.0)
    bwd_routes_keys = jax.random.split(jax.random.fold_in(seeds[9], 1), SECTIONS * TOKENS // TOK_DEV)
    bwd_routes_turns = jax.random.permutation(jax.random.fold_in(seeds[9], 3), SECTIONS * TOKENS // TOK_DEV)
    bwd_routes = jax.vmap(lambda own, number: shared_out(jax.random.fold_in(seeds[9], 2), own, number, TOK_DEV, EXPERTS, TOP, CAP, 2))(bwd_routes_keys, bwd_routes_turns).reshape((SECTIONS, TOKENS, TOP))
    bwd_gates = jnp.clip(0.2 + 0.8 * jax.random.uniform(seeds[10], (SECTIONS, TOKENS, TOP), jnp.float32) ** block_scale(seeds[10], (SECTIONS, TOKENS, TOP), ((0, 8), (1, 32)), -0.2, 0.2), 0.2, 1.0)
    return {"fwd_prev": fwd_prev, "bwd_next": bwd_next, "bwd_input": bwd_input, "norm_gain": norm_gain, "w_gate": w_gate, "w_up": w_up, "w_down": w_down, "fwd_routes": fwd_routes, "fwd_gates": fwd_gates, "bwd_routes": bwd_routes, "bwd_gates": bwd_gates}


EPS = 1e-06

def normalize(hidden_in, gain_vec):
    values = hidden_in.astype(jnp.float32)
    inverse = lax.rsqrt(lax.optimization_barrier(jnp.mean(values * values, axis=-1, keepdims=True)) + EPS)
    normed = (values * inverse * gain_vec).astype(jnp.bfloat16)
    return (values, inverse, normed)

def slot_index(route_block):
    experts_of = route_block.reshape(-1).astype(jnp.int32)
    onehot = (experts_of[:, None] == jnp.arange(EXPERTS, dtype=jnp.int32)[None, :]).astype(jnp.int32)
    before = jnp.cumsum(onehot, axis=0) - onehot
    position = lax.optimization_barrier(jnp.sum(before * onehot, axis=1)).astype(jnp.int32)
    return (experts_of * CAP + position).astype(jnp.int32)

def dispatch_rows(slot_ids, row_data):
    selector = (jnp.arange(EXPERTS * CAP, dtype=jnp.int32)[:, None] == slot_ids[None, :]).astype(row_data.dtype)
    return jnp.dot(selector, row_data, preferred_element_type=jnp.float32).astype(jnp.bfloat16)

def contract_last(left, right):
    return lax.dot_general(left, right, (((1,), (1,)), ((), ())), preferred_element_type=jnp.float32)

def expert_forward(row_data, gate_w, up_w, down_w):
    gate_pre = jnp.dot(row_data, gate_w, preferred_element_type=jnp.float32)
    up_pre = jnp.dot(row_data, up_w, preferred_element_type=jnp.float32)
    hidden = (jax.nn.silu(gate_pre) * up_pre).astype(jnp.bfloat16)
    return jnp.dot(hidden, down_w, preferred_element_type=jnp.float32).astype(jnp.bfloat16)

def expert_backward(row_data, grad_rows, gate_w, up_w, down_w):
    gate_pre = jnp.dot(row_data, gate_w, preferred_element_type=jnp.float32)
    up_pre = jnp.dot(row_data, up_w, preferred_element_type=jnp.float32)
    hidden_grad = contract_last(grad_rows, down_w)
    sig_val = jax.nn.sigmoid(gate_pre)
    gate_grad = (hidden_grad * up_pre * sig_val * (1.0 + gate_pre * (1.0 - sig_val))).astype(jnp.bfloat16)
    up_grad = (hidden_grad * gate_pre * sig_val).astype(jnp.bfloat16)
    input_part = contract_last(gate_grad, gate_w) + contract_last(up_grad, up_w)
    return input_part.astype(jnp.bfloat16)

def collect(returned, slot_ids):
    columns = returned.shape[-1]
    summed = lax.optimization_barrier(jnp.sum(returned.reshape(EXPERTS, -1, CAP, columns).astype(jnp.float32), axis=1))
    return jnp.take(summed.reshape(EXPERTS * CAP, columns), slot_ids, axis=0).reshape(-1, TOP, columns)

def norm_backward(values, inverse, gain_vec, normed_grad, grad_out):
    scaled_grad = normed_grad * gain_vec
    inner_sum = lax.optimization_barrier(jnp.mean(scaled_grad * values, axis=-1, keepdims=True))
    input_grad = grad_out.astype(jnp.float32) + inverse * scaled_grad - values * inverse * inverse * inverse * inner_sum
    return (input_grad.astype(jnp.bfloat16), lax.optimization_barrier(jnp.sum(normed_grad * values * inverse, axis=0)))

def device_weights(w_gate, w_up, w_down):
    gate_dev = w_gate.reshape(D, N_EXPERT, SLICE).transpose(1, 0, 2)
    up_dev = w_up.reshape(D, N_EXPERT, SLICE).transpose(1, 0, 2)
    down_dev = w_down.reshape(N_EXPERT, SLICE, D)
    return (gate_dev, up_dev, down_dev)

def to_experts(buffers):
    return buffers.reshape(N_EXPERT, EXPERTS, CAP, D).transpose(1, 0, 2, 3).reshape(EXPERTS, N_EXPERT * CAP, D)

def to_sources(partials):
    return partials.reshape(N_EXPERT, N_EXPERT, CAP, D).transpose(1, 0, 2, 3)

def forward_section(section_items):
    hidden_in, gain_vec, routes, gates, w_gate, w_up, w_down = section_items
    values, inverse, normed = normalize(hidden_in, gain_vec)
    slot_ids = jax.vmap(slot_index)(routes.reshape(N_EXPERT, TOK_DEV, TOP))
    sources = jnp.repeat(normed.reshape(N_EXPERT, TOK_DEV, D), TOP, axis=1)
    per_expert = to_experts(jax.vmap(dispatch_rows)(slot_ids, sources))
    gate_dev, up_dev, down_dev = device_weights(w_gate, w_up, w_down)

    def one_device(device):
        return expert_forward(per_expert[device // SPLIT], gate_dev[device], up_dev[device], down_dev[device])
    partials = lax.map(one_device, jnp.arange(N_EXPERT, dtype=jnp.int32))
    picked = jax.vmap(collect)(to_sources(partials), slot_ids)
    moe_out = lax.optimization_barrier(jnp.sum(picked * gates.reshape(N_EXPERT, TOK_DEV, TOP, 1), axis=2)).reshape(TOKENS, D)
    return (values + moe_out).astype(jnp.bfloat16)

def backward_section(section_items):
    hidden_in, grad_out, gain_vec, routes, gates, w_gate, w_up, w_down = section_items
    values, inverse, normed = normalize(hidden_in, gain_vec)
    slot_ids = jax.vmap(slot_index)(routes.reshape(N_EXPERT, TOK_DEV, TOP))
    sources = jnp.repeat(normed.reshape(N_EXPERT, TOK_DEV, D), TOP, axis=1)
    scaled = grad_out.astype(jnp.float32).reshape(N_EXPERT, TOK_DEV, 1, D) * gates.reshape(N_EXPERT, TOK_DEV, TOP, 1)
    scaled = scaled.astype(jnp.bfloat16).reshape(N_EXPERT, TOK_DEV * TOP, D)
    norm_expert = to_experts(jax.vmap(dispatch_rows)(slot_ids, sources))
    grad_expert = to_experts(jax.vmap(dispatch_rows)(slot_ids, scaled))
    gate_dev, up_dev, down_dev = device_weights(w_gate, w_up, w_down)

    def one_device(device):
        owner = device // SPLIT
        return expert_backward(norm_expert[owner], grad_expert[owner], gate_dev[device], up_dev[device], down_dev[device])
    partials = lax.map(one_device, jnp.arange(N_EXPERT, dtype=jnp.int32))
    picked = jax.vmap(collect)(to_sources(partials), slot_ids)
    normed_grad = lax.optimization_barrier(jnp.sum(picked, axis=2)).reshape(TOKENS, D)
    return norm_backward(values, inverse, gain_vec, normed_grad, grad_out)

def reference(fwd_prev, bwd_next, bwd_input, norm_gain, w_gate, w_up, w_down, fwd_routes, fwd_gates, bwd_routes, bwd_gates):
    fwd_in = jnp.roll(fwd_prev, 1, axis=0)
    grad_in = jnp.roll(bwd_next, -1, axis=0)
    fwd_out = lax.map(forward_section, (fwd_in, norm_gain, fwd_routes, fwd_gates, w_gate, w_up, w_down))
    bwd_grad, gain_grad = lax.map(backward_section, (bwd_input, grad_in, norm_gain, bwd_routes, bwd_gates, w_gate, w_up, w_down))
    return (fwd_out, bwd_grad, gain_grad)
```

```python
import jax
import jax.numpy as jnp
from jax import lax
from jax.experimental import pallas as pl
from jax.experimental.pallas import tpu as pltpu
from jax.sharding import PartitionSpec as P

MESH = pl.DeviceIdType.MESH
F32 = jnp.float32
BF16 = jnp.bfloat16

EPS = 1e-06
D = 3584
HALF = D // 2
TOK = 128
CAP = 24
ROWS = 2 * CAP
SLICE = 256
SLOTS = 8
GROUPS = SLOTS // 2
PIPE = 8

XB, DY, XF = 0, 1, 2
BWD, FWD = 0, 1

S_META = 0
S_WEIGHT = 9
S_RING = 12
S_PAIR = 36
S_DUP = 40
S_PART = 56
S_BACK = 64
S_GAIN = 80
N_SEM = 90


def dot(left, right):
    return jnp.dot(left, right, preferred_element_type=F32)


def contract_last(left, right):
    return lax.dot_general(left, right, (((1,), (1,)), ((), ())), preferred_element_type=F32)


def iota(shape, dim):
    return lax.broadcasted_iota(jnp.int32, shape, dim).astype(F32)


def halves(chunk):
    values = chunk.astype(F32)
    return values[:CAP], values[CAP:]


def inverse_rms(left, right):
    total = jnp.sum(left * left, axis=-1, keepdims=True)
    total = total + jnp.sum(right * right, axis=-1, keepdims=True)
    return lax.rsqrt(total * (1.0 / D) + EPS)


def earlier():
    return (iota((TOK, TOK), 0) < iota((TOK, TOK), 1)).astype(BF16)


def places(routes, z):
    onehot = (iota((8, TOK), 0) == routes).astype(F32)
    before = dot(onehot.astype(BF16), earlier())
    position = jnp.sum(onehot * before, axis=0, keepdims=True)
    ahead = routes - z.astype(F32)
    ahead = jnp.where(ahead < 0, ahead + 8, ahead)
    slot = jnp.where(ahead <= 4, 2 * ahead - 1, 2 * (8 - ahead))
    slot = jnp.where(ahead == 0, 0.0, slot)
    return slot * ROWS + position


def kernel(
    meta,
    gain,
    x_hbm,
    dy_hbm,
    xb_hbm,
    wg_hbm,
    wu_hbm,
    wd_hbm,
    of_hbm,
    ob_hbm,
    og_ref,
    raw,
    sent,
    landed,
    pair_xb,
    all_dy,
    all_x,
    part_out,
    part_in,
    own_part,
    final,
    back,
    outs,
    wg,
    wu,
    wd,
    normed,
    grads,
    acc,
    ring_meta,
    near_meta,
    gain_acc,
    gain_ring,
    gain_sum,
    gain_near,
    send_sem,
    recv_sem,
    local_sem,
):
    pipe = lax.axis_index("pipe")
    place = lax.axis_index("expert")
    z = place // 4
    xh = (place // 2) % 2
    core = place % 2

    def at_ring(offset):
        return {"pipe": pipe, "expert": lax.rem(z + offset + 8, 8) * 4 + xh * 2 + core}

    pair = {"pipe": pipe, "expert": z * 4 + (1 - xh) * 2 + core}
    twin = {"pipe": pipe, "expert": z * 4 + xh * 2 + (1 - core)}

    def at_section(distance, other):
        side = (1 - xh) if other else xh
        return {"pipe": lax.rem(pipe + distance + PIPE, PIPE), "expert": z * 4 + side * 2 + core}

    def remote(src, dst, sem, device):
        return pltpu.make_async_remote_copy(
            src_ref=src,
            dst_ref=dst,
            send_sem=send_sem.at[sem],
            recv_sem=recv_sem.at[sem],
            device_id=device,
            device_id_type=MESH,
        )

    loads = []
    for array, hbm in ((XB, xb_hbm), (DY, dy_hbm), (XF, x_hbm)):
        for half in range(2):
            loads.append(
                pltpu.make_async_copy(
                    hbm.at[0, :, pl.ds(half * HALF, HALF)],
                    raw.at[array, pl.ds(half * TOK, TOK)],
                    local_sem.at[array * 2 + half],
                )
            )
    for index, (hbm, vmem) in enumerate(((wg_hbm, wg), (wu_hbm, wu), (wd_hbm, wd))):
        loads.append(pltpu.make_async_copy(hbm.at[0], vmem.at[0], local_sem.at[6 + index]))
    for load in loads:
        load.start()

    barrier = pltpu.get_barrier_semaphore()
    partners = [at_ring(k) for k in range(1, 8)] + [pair, twin]
    for distance in (-1, 1):
        partners += [at_section(distance, False), at_section(distance, True)]
    for device in partners:
        pl.semaphore_signal(barrier, inc=1, device_id=device, device_id_type=MESH)
    pl.semaphore_wait(barrier, len(partners))

    def offset_of(slot):
        return (slot + 1) // 2 if slot % 2 else -(slot // 2)

    metas = [
        remote(meta, near_meta.at[0], S_META, at_section(-1, False)),
        remote(meta, near_meta.at[1], S_META + 1, at_section(1, False)),
    ]
    for slot in range(1, SLOTS):
        metas.append(
            remote(meta, ring_meta.at[slot], S_META + 1 + slot, at_ring(offset_of(slot)))
        )
    for copy in metas:
        copy.start()
    ring_meta[0] = meta[...]

    weights = [
        remote(hbm.at[0], vmem.at[1], S_WEIGHT + index, twin)
        for index, (hbm, vmem) in enumerate(((wg_hbm, wg), (wu_hbm, wu), (wd_hbm, wd)))
    ]

    def ring_copy(array, slot, offset):
        return remote(
            sent.at[array, slot],
            landed.at[array, slot],
            S_RING + array * 8 + slot,
            at_ring(offset),
        )

    def dispatch(array, routes):
        base = places(routes, z)

        def step(group, carry):
            row = iota((2 * ROWS, TOK), 0) + (group * (2 * ROWS)).astype(F32)
            picks = jnp.concatenate([row == base, row == base + CAP], axis=1)
            picks = picks.astype(F32).astype(BF16)
            rows = dot(picks, raw[array]).astype(BF16)
            sent[array, pl.ds(2 * group, 2)] = rows.reshape(2, ROWS, HALF)
            ring_copy(array, 2 * group + 1, group + 1).start()

            @pl.when(group > 0)
            def _():
                ring_copy(array, 2 * group, -group).start()

            return carry

        lax.fori_loop(0, GROUPS, step, 0)
        landed[array, 0] = sent[array, 0]

    def wait_landed(array, group):
        ring_copy(array, 2 * group + 1, group + 1).wait_recv()

        @pl.when(group > 0)
        def _():
            ring_copy(array, 2 * group, -group).wait_recv()

    loads[0].wait()
    loads[1].wait()
    dispatch(XB, meta[2:3, :])
    for copy in weights:
        copy.start()
    metas[1].wait_recv()
    loads[2].wait()
    loads[3].wait()
    dispatch(DY, near_meta[1, 2:3, :])
    metas[0].wait_recv()
    loads[4].wait()
    loads[5].wait()
    dispatch(XF, near_meta[0, 0:1, :])

    def pair_copy(group):
        two = pl.ds(2 * group, 2)
        return remote(landed.at[XB, two], pair_xb.at[two], S_PAIR + group, pair)

    def dup_copy(array, group, other):
        two = pl.ds(2 * group, 2)
        dst = all_dy if array == DY else all_x
        sem = S_DUP + (array - 1) * 8 + other * 4 + group
        device = at_section(-1 if array == DY else 1, other)
        return remote(landed.at[array, two], dst.at[other, two], sem, device)

    def relay_pair(group, carry):
        wait_landed(XB, group)
        pair_copy(group).start()
        return carry

    def relay_dup(array, group):
        wait_landed(array, group)
        dup_copy(array, group, 0).start()
        dup_copy(array, group, 1).start()

    def relay_dy(group, carry):
        relay_dup(DY, group)
        return carry

    lax.fori_loop(0, GROUPS, relay_pair, 0)
    lax.fori_loop(0, GROUPS, relay_dy, 0)

    gain_left = gain[:, :HALF]
    gain_right = gain[:, HALF:]

    def gather_rows(own, other, group, to, scaled):
        for side, ref in enumerate((own, other)):
            lefts, rights = [], []
            for s in range(2):
                left, right = halves(ref(2 * group + s))
                if scaled:
                    inverse = inverse_rms(left, right)
                    left = left * inverse * gain_left
                    right = right * inverse * gain_right
                lefts.append(left)
                rights.append(right)
            rows = pl.ds(side * ROWS, ROWS)
            to[rows, pl.ds(0, HALF)] = jnp.concatenate(lefts, axis=0).astype(BF16)
            to[rows, pl.ds(HALF, HALF)] = jnp.concatenate(rights, axis=0).astype(BF16)

    def part_copy(which, group):
        two = pl.ds(2 * group, 2)
        return remote(
            part_out.at[which, two], part_in.at[which, two], S_PART + which * 4 + group, pair
        )

    def share(which, group):
        own_part[which, group] = acc[pl.ds(0, ROWS), :]
        for s in range(2):
            rows = pl.ds(ROWS + s * CAP, CAP)
            chunk = jnp.concatenate([acc[rows, pl.ds(0, HALF)], acc[rows, pl.ds(HALF, HALF)]], axis=0)
            part_out[which, 2 * group + s] = chunk.astype(BF16)
        part_copy(which, group).start()

    for load in loads[6:]:
        load.wait()
    for copy in weights:
        copy.wait_recv()

    def backward(group, carry):
        relay_dup(XF, group)
        pair_copy(group).wait_recv()
        dup_copy(DY, group, 0).wait_recv()
        dup_copy(DY, group, 1).wait_recv()
        gather_rows(
            lambda j: landed[XB, j], lambda j: pair_xb[j], group, normed, True
        )
        gather_rows(lambda j: all_dy[0, j], lambda j: all_dy[1, j], group, grads, False)
        acc[...] = jnp.zeros_like(acc)

        def hidden(h, inner):
            rows = normed[...]
            a = dot(rows, wg[h])
            b = dot(rows, wu[h])
            dh = contract_last(grads[...], wd[h])
            sig = 1.0 / (1.0 + jnp.exp(-a))
            da = (dh * b * sig * (1.0 + a * (1.0 - sig))).astype(BF16)
            db = (dh * a * sig).astype(BF16)
            acc[...] += contract_last(da, wg[h]) + contract_last(db, wu[h])
            return inner

        lax.fori_loop(0, 2, hidden, 0)
        share(BWD, group)
        return carry

    lax.fori_loop(0, GROUPS, backward, 0)

    def gates_of(which, slot):
        routes = ring_meta[slot, pl.ds(2 * (1 - which), 1), :]
        gates = ring_meta[slot, pl.ds(2 * (1 - which) + 1, 1), :]
        mine = (routes == z.astype(F32)).astype(F32)
        before = dot(jnp.broadcast_to(mine, (8, TOK)).astype(BF16), earlier())[0:1]
        chosen = jnp.where(mine > 0, before, -1.0)
        picked = jnp.where(iota((CAP, TOK), 0) == chosen, gates, 0.0)
        return jnp.sum(picked, axis=1, keepdims=True)

    def back_copy(which, slot, offset):
        return remote(
            final.at[which, slot],
            back.at[which, slot],
            S_BACK + which * 8 + slot,
            at_ring(-offset),
        )

    def send_back(which, group):
        back_copy(which, 2 * group + 1, group + 1).start()

        @pl.when(group > 0)
        def _():
            back_copy(which, 2 * group, -group).start()

        @pl.when(group == 0)
        def _():
            back[which, 0] = final[which, 0]

    def summed(which, group, s):
        rows = pl.ds(s * CAP, CAP)
        left, right = halves(part_in[which, 2 * group + s])
        gate = gates_of(which, 2 * group + s)
        left = gate * (left + own_part[which, group, rows, pl.ds(0, HALF)])
        right = gate * (right + own_part[which, group, rows, pl.ds(HALF, HALF)])
        return left, right

    for copy in metas[2:]:
        copy.wait_recv()
    gain_acc[...] = jnp.zeros_like(gain_acc)

    def finish_backward(group):
        part_copy(BWD, group).wait_recv()
        for s in range(2):
            slot = 2 * group + s
            dn_left, dn_right = summed(BWD, group, s)
            x_left, x_right = halves(landed[XB, slot])
            inverse = inverse_rms(x_left, x_right)
            u_left = dn_left * gain_left
            u_right = dn_right * gain_right
            inner = jnp.sum(u_left * x_left, axis=-1, keepdims=True)
            inner = inner + jnp.sum(u_right * x_right, axis=-1, keepdims=True)
            scale = inverse * inverse * inverse * (inner * (1.0 / D))
            dy_left, dy_right = halves(all_dy[0, slot])
            g_left = dy_left + inverse * u_left - x_left * scale
            g_right = dy_right + inverse * u_right - x_right * scale
            final[BWD, slot] = jnp.concatenate([g_left, g_right], axis=0).astype(BF16)
            gain_acc[:, pl.ds(0, HALF)] += jnp.sum(
                dn_left * x_left * inverse, axis=0, keepdims=True
            )
            gain_acc[:, pl.ds(HALF, HALF)] += jnp.sum(
                dn_right * x_right * inverse, axis=0, keepdims=True
            )
        send_back(BWD, group)

    def forward(group, carry):
        dup_copy(XF, group, 0).wait_recv()
        dup_copy(XF, group, 1).wait_recv()
        gather_rows(lambda j: all_x[0, j], lambda j: all_x[1, j], group, normed, True)
        acc[...] = jnp.zeros_like(acc)

        def hidden(h, inner):
            rows = normed[...]
            a = dot(rows, wg[h])
            b = dot(rows, wu[h])
            act = (a / (1.0 + jnp.exp(-a)) * b).astype(BF16)
            acc[...] += dot(act, wd[h])
            return inner

        lax.fori_loop(0, 2, hidden, 0)
        share(FWD, group)
        finish_backward(group)
        return carry

    lax.fori_loop(0, GROUPS, forward, 0)

    gain_sum[0] = jnp.zeros((32, 128), F32)
    for r in range(28):
        gain_sum[0, r : r + 1, :] = gain_acc[:, r * 128 : (r + 1) * 128]
    gain_ring[z] = gain_sum[0]
    gain_copies = [
        remote(gain_sum.at[0], gain_ring.at[z], S_GAIN + slot, at_ring(offset_of(slot)))
        for slot in range(1, SLOTS)
    ]
    for copy in gain_copies:
        copy.start()

    def finish_forward(group, carry):
        part_copy(FWD, group).wait_recv()
        for s in range(2):
            slot = 2 * group + s
            q_left, q_right = summed(FWD, group, s)
            x_left, x_right = halves(all_x[0, slot])
            chunk = jnp.concatenate([x_left + q_left, x_right + q_right], axis=0)
            final[FWD, slot] = chunk.astype(BF16)
        send_back(FWD, group)
        return carry

    lax.fori_loop(0, GROUPS, finish_forward, 0)

    for copy in gain_copies:
        copy.wait_recv()
    total = gain_ring[0]
    for index in range(1, 8):
        total = total + gain_ring[index]
    gain_sum[1] = total
    twin_copy = remote(gain_sum.at[1], gain_near.at[0], S_GAIN + 8, twin)
    twin_copy.start()

    stores = []

    def collect(which, hbm, routes):
        for slot in range(1, SLOTS):
            back_copy(which, slot, offset_of(slot)).wait_recv()
        base = jnp.broadcast_to(places(routes, z), (TOK, TOK)).T[:, 0:1]
        column = iota((TOK, SLOTS * ROWS), 1)
        picks = jnp.concatenate([column == base, column == base + CAP], axis=0)
        picks = picks.astype(F32).astype(BF16)
        rows = dot(picks, back[which].reshape(SLOTS * ROWS, HALF))
        outs[which] = rows.astype(BF16)
        for half in range(2):
            store = pltpu.make_async_copy(
                outs.at[which, pl.ds(half * TOK, TOK)],
                hbm.at[0, :, pl.ds(half * HALF, HALF)],
                local_sem.at[9 + which * 2 + half],
            )
            store.start()
            stores.append(store)

    collect(BWD, ob_hbm, meta[2:3, :])
    twin_copy.wait_recv()
    gain_sum[2] = gain_sum[1] + gain_near[0]
    pair_sum = remote(gain_sum.at[2], gain_near.at[1], S_GAIN + 9, pair)
    pair_sum.start()
    collect(FWD, of_hbm, meta[0:1, :])
    pair_sum.wait_recv()
    og_ref[...] = gain_sum[2] + gain_near[1]

    for copy in metas + weights + gain_copies + [twin_copy, pair_sum]:
        copy.wait_send()

    def sent_all(group, carry):
        for array in (XB, DY, XF):
            ring_copy(array, 2 * group + 1, group + 1).wait_send()
        for which in (BWD, FWD):
            back_copy(which, 2 * group + 1, group + 1).wait_send()
            part_copy(which, group).wait_send()

        @pl.when(group > 0)
        def _():
            for array in (XB, DY, XF):
                ring_copy(array, 2 * group, -group).wait_send()
            for which in (BWD, FWD):
                back_copy(which, 2 * group, -group).wait_send()

        pair_copy(group).wait_send()
        for array in (DY, XF):
            for other in range(2):
                dup_copy(array, group, other).wait_send()
        return carry

    lax.fori_loop(0, GROUPS, sent_all, 0)
    for store in stores:
        store.wait()


def chunks(*lead):
    return pltpu.VMEM((*lead, SLOTS, ROWS, HALF), BF16)


def body(
    fwd_prev,
    bwd_next,
    bwd_input,
    norm_gain,
    w_gate,
    w_up,
    w_down,
    fwd_routes,
    fwd_gates,
    bwd_routes,
    bwd_gates,
):
    lines = [
        fwd_routes.astype(F32).reshape(1, TOK),
        fwd_gates.reshape(1, TOK),
        bwd_routes.astype(F32).reshape(1, TOK),
        bwd_gates.reshape(1, TOK),
        jnp.zeros((4, TOK), F32),
    ]
    meta = jnp.concatenate(lines, axis=0)
    vmem = pl.BlockSpec(memory_space=pltpu.VMEM)
    anywhere = pl.BlockSpec(memory_space=pl.ANY)
    fwd_out, bwd_grad, gain_grad = pl.pallas_call(
        kernel,
        out_shape=(
            jax.ShapeDtypeStruct(fwd_prev.shape, BF16),
            jax.ShapeDtypeStruct(fwd_prev.shape, BF16),
            jax.ShapeDtypeStruct((32, 128), F32),
        ),
        in_specs=[vmem] * 2 + [anywhere] * 6,
        out_specs=(anywhere, anywhere, vmem),
        scratch_shapes=[
            pltpu.VMEM((3, 2 * TOK, HALF), BF16),
            chunks(3),
            chunks(3),
            chunks(),
            chunks(2),
            chunks(2),
            chunks(2),
            chunks(2),
            pltpu.VMEM((2, GROUPS, ROWS, D), F32),
            chunks(2),
            chunks(2),
            pltpu.VMEM((2, 2 * TOK, HALF), BF16),
            pltpu.VMEM((2, D, SLICE), BF16),
            pltpu.VMEM((2, D, SLICE), BF16),
            pltpu.VMEM((2, SLICE, D), BF16),
            pltpu.VMEM((2 * ROWS, D), BF16),
            pltpu.VMEM((2 * ROWS, D), BF16),
            pltpu.VMEM((2 * ROWS, D), F32),
            pltpu.VMEM((SLOTS, 8, TOK), F32),
            pltpu.VMEM((2, 8, TOK), F32),
            pltpu.VMEM((1, D), F32),
            pltpu.VMEM((8, 32, 128), F32),
            pltpu.VMEM((3, 32, 128), F32),
            pltpu.VMEM((2, 32, 128), F32),
            pltpu.SemaphoreType.DMA((N_SEM,)),
            pltpu.SemaphoreType.DMA((N_SEM,)),
            pltpu.SemaphoreType.DMA((13,)),
        ],
        compiler_params=pltpu.CompilerParams(
            collective_id=0, has_side_effects=True, vmem_limit_bytes=62 * 2**20
        ),
    )(meta, norm_gain, fwd_prev, bwd_next, bwd_input, w_gate, w_up, w_down)
    return (fwd_out, bwd_grad, gain_grad[:28].reshape(1, D))


def solution(mesh):
    rows = P("pipe", "expert", None)
    columns = P("pipe", None, "expert")
    placed = (rows, rows, rows, P("pipe", None), columns, columns, rows, rows, rows, rows, rows)
    return jax.shard_map(
        body,
        mesh=mesh,
        in_specs=placed,
        out_specs=(rows, rows, P("pipe", None)),
        check_vma=False,
    )
```

```python
import jax
import jax.numpy as jnp
from jax import lax
from jax.experimental import pallas as pl
from jax.experimental.pallas import tpu as pltpu
from jax.sharding import PartitionSpec as P

MESH = pl.DeviceIdType.MESH
F32 = jnp.float32
BF16 = jnp.bfloat16

EPS = 1e-06
D = 3584
HALF = D // 2
TOK = 128
CAP = 24
ROWS = 2 * CAP
SLICE = 256
STAY = 2
SLOTS = 8
GROUPS = SLOTS // 2
PIPE = 8

XB, DY, XF = 0, 1, 2
BWD, FWD = 0, 1

S_META = 0
S_WEIGHT = 9
S_RING = 12
S_PAIR = 36
S_DUP = 40
S_PART = 56
S_BACK = 64
S_GAIN = 80
S_META_RING = 90
N_SEM = 98


def dot(left, right):
    return jnp.dot(left, right, preferred_element_type=F32)


def contract_last(left, right):
    return lax.dot_general(left, right, (((1,), (1,)), ((), ())), preferred_element_type=F32)


def iota(shape, dim):
    return lax.broadcasted_iota(jnp.int32, shape, dim).astype(F32)


def halves(chunk):
    values = chunk.astype(F32)
    return values[:CAP], values[CAP:]


def inverse_rms(left, right):
    total = jnp.sum(left * left, axis=-1, keepdims=True)
    total = total + jnp.sum(right * right, axis=-1, keepdims=True)
    return lax.rsqrt(total * (1.0 / D) + EPS)


def earlier():
    return (iota((TOK, TOK), 0) < iota((TOK, TOK), 1)).astype(BF16)


def places(routes, z):
    onehot = (iota((8, TOK), 0) == routes).astype(F32)
    before = dot(onehot.astype(BF16), earlier())
    position = jnp.sum(onehot * before, axis=0, keepdims=True)
    ahead = routes - z.astype(F32)
    ahead = jnp.where(ahead < 0, ahead + 8, ahead)
    near = jnp.minimum(ahead, 8 - ahead)
    group = jnp.where(near == 2, 0.0, jnp.where(near == 3, 2.0, jnp.where(near == 1, 3.0, 1.0)))
    slot = 2 * group + jnp.where(ahead >= 4, 1.0, 0.0)
    return slot * ROWS + position


def offsets(group):
    first = (2 + 3 * group) % 5
    return first, 4 * ((4 - first) // 4) - first


def kernel(
    routes_f,
    gates_f,
    routes_b,
    gates_b,
    gain,
    x_hbm,
    dy_hbm,
    xb_hbm,
    wg_hbm,
    wu_hbm,
    wd_hbm,
    of_hbm,
    ob_hbm,
    og_ref,
    raw,
    sent,
    landed,
    pair_xb,
    all_dy,
    all_x,
    part_out,
    part_in,
    own_part,
    final,
    back,
    outs,
    wg,
    wu,
    wd,
    normed,
    grads,
    acc,
    meta,
    ring_meta,
    near_meta,
    gain_acc,
    gain_ring,
    gain_sum,
    gain_near,
    picked,
    send_sem,
    recv_sem,
    local_sem,
):
    pipe = lax.axis_index("pipe")
    place = lax.axis_index("expert")
    z = place // 4
    xh = (place // 2) % 2
    core = place % 2
    odd = pipe % 2
    even = 1 - odd

    def at_ring(offset, ahead=0):
        return {
            "pipe": lax.rem(pipe + ahead + PIPE, PIPE),
            "expert": lax.rem(z + offset + 8, 8) * 4 + xh * 2 + core,
        }

    pair = {"pipe": pipe, "expert": z * 4 + (1 - xh) * 2 + core}
    twin = {"pipe": pipe, "expert": z * 4 + xh * 2 + (1 - core)}

    def at_section(distance):
        return {"pipe": lax.rem(pipe + distance + PIPE, PIPE), "expert": place}

    def beside(other):
        side = (1 - xh) if other else xh
        return {"pipe": pipe + 1 - 2 * odd, "expert": z * 4 + side * 2 + core}

    def remote(src, dst, sem, device):
        return pltpu.make_async_remote_copy(
            src_ref=src,
            dst_ref=dst,
            send_sem=send_sem.at[sem],
            recv_sem=recv_sem.at[sem],
            device_id=device,
            device_id_type=MESH,
        )

    loads = []
    for array, hbm in ((XB, xb_hbm), (DY, dy_hbm), (XF, x_hbm)):
        for half in range(2):
            loads.append(
                pltpu.make_async_copy(
                    hbm.at[0, :, pl.ds(half * HALF, HALF)],
                    raw.at[array, pl.ds(half * TOK, TOK)],
                    local_sem.at[array * 2 + half],
                )
            )
    for index, (hbm, vmem) in enumerate(((wg_hbm, wg), (wu_hbm, wu), (wd_hbm, wd))):
        loads.append(pltpu.make_async_copy(hbm.at[0], vmem.at[0], local_sem.at[6 + index]))
    for load in loads:
        load.start()

    barrier = pltpu.get_barrier_semaphore()
    partners = [at_ring(k) for k in range(1, 8)] + [pair, twin]
    partners += [beside(0), beside(1), at_section(2 * odd - 1)]
    partners += [at_ring(k, ahead) for ahead in (-2, 2) for k in range(8)]
    for device in partners:
        pl.semaphore_signal(barrier, inc=1, device_id=device, device_id_type=MESH)

    meta[...] = jnp.zeros_like(meta)
    for line, ref in enumerate((routes_f, gates_f, routes_b, gates_b)):
        meta[line : line + 1, :] = ref[...].astype(F32)

    def offset_of(slot):
        return offsets(slot // 2)[slot % 2]

    others = [slot for slot in range(SLOTS) if offset_of(slot)]

    metas = [
        remote(meta, near_meta.at[0], S_META, at_section(-1)),
        remote(meta, near_meta.at[1], S_META + 1, at_section(1)),
    ]
    for slot in others:
        metas.append(
            remote(meta, ring_meta.at[slot], S_META_RING + slot, at_ring(offset_of(slot)))
        )
    weights = [
        remote(hbm.at[0], vmem.at[1], S_WEIGHT + index, twin)
        for index, (hbm, vmem) in enumerate(((wg_hbm, wg), (wu_hbm, wu), (wd_hbm, wd)))
    ]

    ahead_of = (0, -2 * even, 2 * odd)

    def ring_copy(array, slot, offset):
        return remote(
            sent.at[array, slot],
            landed.at[array, slot],
            S_RING + array * 8 + slot,
            at_ring(offset, ahead_of[array]),
        )

    def each_ring(array, group, act, stay=lambda: None):
        one, two = offsets(group)
        act(ring_copy(array, 2 * group + 1, two))
        moved = (0, even, odd)[array]
        goes = (one != 0) if array == XB else (one != 0) | (moved == 1)

        @pl.when(goes)
        def _():
            act(ring_copy(array, 2 * group, one))

        @pl.when(jnp.logical_not(goes))
        def _():
            stay()

    def prepare(array, routes):
        base = places(routes, z)

        def step(group, carry):
            row = iota((2 * ROWS, TOK), 0) + (group * (2 * ROWS)).astype(F32)
            picks = jnp.concatenate([row == base, row == base + CAP], axis=1)
            picks = picks.astype(F32).astype(BF16)
            rows = dot(picks, raw[array]).astype(BF16)
            sent[array, pl.ds(2 * group, 2)] = rows.reshape(2, ROWS, HALF)
            return carry

        lax.fori_loop(0, GROUPS, step, 0)

    def send_group(array, group):
        def keep():
            landed[array, STAY] = sent[array, STAY]

        each_ring(array, group, lambda copy: copy.start(), keep)

    def wait_landed(array, group):
        each_ring(array, group, lambda copy: copy.wait_recv())

    loads[0].wait()
    loads[1].wait()
    prepare(XB, meta[2:3, :])
    pl.semaphore_wait(barrier, len(partners))
    for group in (3, 0, 1, 2):
        send_group(XB, group)
    for copy in metas + weights:
        copy.start()
    ring_meta[STAY] = meta[...]
    metas[1].wait_recv()
    loads[2].wait()
    loads[3].wait()
    prepare(DY, near_meta[1, 2:3, :])

    def pair_copy(group):
        two = pl.ds(2 * group, 2)
        return remote(landed.at[XB, two], pair_xb.at[two], S_PAIR + group, pair)

    def dup_copy(array, group, other):
        two = pl.ds(2 * group, 2)
        dst = all_dy if array == DY else all_x
        sem = S_DUP + (array - 1) * 8 + other * 4 + group
        return remote(landed.at[array, two], dst.at[other, two], sem, beside(other))

    def relay_pair(group):
        wait_landed(XB, group)
        pair_copy(group).start()

    def relay_dup(array, group):
        wait_landed(array, group)
        dup_copy(array, group, 0).start()
        dup_copy(array, group, 1).start()

    def prepare_collect(which, routes):
        base = jnp.broadcast_to(places(routes, z), (TOK, TOK)).T[:, 0:1]
        column = iota((TOK, SLOTS * ROWS), 1)
        picks = jnp.concatenate([column == base, column == base + CAP], axis=0)
        picked[which] = picks.astype(F32).astype(BF16)

    relay_pair(3)
    relay_pair(0)
    send_group(DY, 0)
    send_group(DY, 1)
    send_group(DY, 2)
    send_group(DY, 3)
    metas[0].wait_recv()
    loads[4].wait()
    loads[5].wait()
    prepare(XF, near_meta[0, 0:1, :])
    relay_pair(1)
    relay_pair(2)
    relay_dup(DY, 0)
    relay_dup(DY, 1)
    send_group(XF, 0)
    send_group(XF, 1)
    send_group(XF, 2)
    send_group(XF, 3)
    relay_dup(DY, 2)
    relay_dup(DY, 3)

    prepare_collect(FWD, meta[0:1, :])
    prepare_collect(BWD, meta[2:3, :])

    gain_left = gain[:, :HALF]
    gain_right = gain[:, HALF:]

    def gather_rows(own, other, group, to, scaled):
        for side, ref in enumerate((own, other)):
            lefts, rights = [], []
            for s in range(2):
                left, right = halves(ref(2 * group + s))
                if scaled:
                    inverse = inverse_rms(left, right)
                    left = left * inverse * gain_left
                    right = right * inverse * gain_right
                lefts.append(left)
                rights.append(right)
            rows = pl.ds(side * ROWS, ROWS)
            to[rows, pl.ds(0, HALF)] = jnp.concatenate(lefts, axis=0).astype(BF16)
            to[rows, pl.ds(HALF, HALF)] = jnp.concatenate(rights, axis=0).astype(BF16)

    def part_copy(which, group):
        two = pl.ds(2 * group, 2)
        return remote(
            part_out.at[which, two], part_in.at[which, two], S_PART + which * 4 + group, pair
        )

    def share(which, group):
        own_part[which, group] = acc[pl.ds(0, ROWS), :]
        for s in range(2):
            rows = pl.ds(ROWS + s * CAP, CAP)
            chunk = jnp.concatenate([acc[rows, pl.ds(0, HALF)], acc[rows, pl.ds(HALF, HALF)]], axis=0)
            part_out[which, 2 * group + s] = chunk.astype(BF16)
        part_copy(which, group).start()

    for load in loads[6:]:
        load.wait()
    for copy in weights:
        copy.wait_recv()

    def gates_of(which, slot):
        routes = ring_meta[slot, pl.ds(2 * (1 - which), 1), :]
        gates = ring_meta[slot, pl.ds(2 * (1 - which) + 1, 1), :]
        mine = (routes == z.astype(F32)).astype(F32)
        before = dot(jnp.broadcast_to(mine, (8, TOK)).astype(BF16), earlier())[0:1]
        chosen = jnp.where(mine > 0, before, -1.0)
        picked = jnp.where(iota((CAP, TOK), 0) == chosen, gates, 0.0)
        return jnp.sum(picked, axis=1, keepdims=True)

    def back_copy(which, slot, offset):
        return remote(
            final.at[which, slot],
            back.at[which, slot],
            S_BACK + which * 8 + slot,
            at_ring(-offset),
        )

    def each_back(which, group, act, stay=lambda: None):
        one, two = offsets(group)
        act(back_copy(which, 2 * group + 1, two))

        @pl.when(one != 0)
        def _():
            act(back_copy(which, 2 * group, one))

        @pl.when(one == 0)
        def _():
            stay()

    def send_back(which, group):
        def keep():
            back[which, STAY] = final[which, STAY]

        each_back(which, group, lambda copy: copy.start(), keep)

    def summed(which, group, s):
        rows = pl.ds(s * CAP, CAP)
        left, right = halves(part_in[which, 2 * group + s])
        gate = gates_of(which, 2 * group + s)
        left = gate * (left + own_part[which, group, rows, pl.ds(0, HALF)])
        right = gate * (right + own_part[which, group, rows, pl.ds(HALF, HALF)])
        return left, right

    def finish_forward(group):
        part_copy(FWD, group).wait_recv()
        for s in range(2):
            slot = 2 * group + s
            q_left, q_right = summed(FWD, group, s)
            x_left, x_right = halves(all_x[0, slot])
            chunk = jnp.concatenate([x_left + q_left, x_right + q_right], axis=0)
            final[FWD, slot] = chunk.astype(BF16)
        send_back(FWD, group)

    gain_acc[...] = jnp.zeros_like(gain_acc)

    def finish_backward(group):
        part_copy(BWD, group).wait_recv()
        for s in range(2):
            slot = 2 * group + s
            dn_left, dn_right = summed(BWD, group, s)
            x_left, x_right = halves(landed[XB, slot])
            inverse = inverse_rms(x_left, x_right)
            u_left = dn_left * gain_left
            u_right = dn_right * gain_right
            inner = jnp.sum(u_left * x_left, axis=-1, keepdims=True)
            inner = inner + jnp.sum(u_right * x_right, axis=-1, keepdims=True)
            scale = inverse * inverse * inverse * (inner * (1.0 / D))
            dy_left, dy_right = halves(all_dy[0, slot])
            g_left = dy_left + inverse * u_left - x_left * scale
            g_right = dy_right + inverse * u_right - x_right * scale
            final[BWD, slot] = jnp.concatenate([g_left, g_right], axis=0).astype(BF16)
            gain_acc[:, pl.ds(0, HALF)] += jnp.sum(
                dn_left * x_left * inverse, axis=0, keepdims=True
            )
            gain_acc[:, pl.ds(HALF, HALF)] += jnp.sum(
                dn_right * x_right * inverse, axis=0, keepdims=True
            )
        send_back(BWD, group)

    def backward(group, carry):
        pair_copy(group).wait_recv()
        dup_copy(DY, group, 0).wait_recv()
        dup_copy(DY, group, 1).wait_recv()
        gather_rows(
            lambda j: landed[XB, j], lambda j: pair_xb[j], group, normed, True
        )
        gather_rows(lambda j: all_dy[0, j], lambda j: all_dy[1, j], group, grads, False)
        acc[...] = jnp.zeros_like(acc)

        def hidden(h, inner):
            rows = normed[...]
            a = dot(rows, wg[h])
            b = dot(rows, wu[h])
            dh = contract_last(grads[...], wd[h])
            sig = 1.0 / (1.0 + jnp.exp(-a))
            da = (dh * b * sig * (1.0 + a * (1.0 - sig))).astype(BF16)
            db = (dh * a * sig).astype(BF16)
            acc[...] += contract_last(da, wg[h]) + contract_last(db, wu[h])
            return inner

        lax.fori_loop(0, 2, hidden, 0)
        share(BWD, group)
        relay_dup(XF, group)

        return carry

    lax.fori_loop(0, GROUPS, backward, 0)

    for copy in metas[2:]:
        copy.wait_recv()

    def forward(group, carry):
        dup_copy(XF, group, 0).wait_recv()
        dup_copy(XF, group, 1).wait_recv()
        gather_rows(lambda j: all_x[0, j], lambda j: all_x[1, j], group, normed, True)
        acc[...] = jnp.zeros_like(acc)

        def hidden(h, inner):
            rows = normed[...]
            a = dot(rows, wg[h])
            b = dot(rows, wu[h])
            act = (a / (1.0 + jnp.exp(-a)) * b).astype(BF16)
            acc[...] += dot(act, wd[h])
            return inner

        lax.fori_loop(0, 2, hidden, 0)
        share(FWD, group)
        finish_backward(group)
        return carry

    lax.fori_loop(0, GROUPS, forward, 0)


    gain_sum[0] = jnp.zeros((32, 128), F32)
    for r in range(28):
        gain_sum[0, r : r + 1, :] = gain_acc[:, r * 128 : (r + 1) * 128]
    gain_ring[z] = gain_sum[0]
    gain_copies = [
        remote(gain_sum.at[0], gain_ring.at[z], S_GAIN + slot, at_ring(offset_of(slot)))
        for slot in others
    ]
    for copy in gain_copies:
        copy.start()

    for copy in metas + weights:
        copy.wait_send()

    def first_sent(group, carry):
        for array in (XB, DY, XF):
            each_ring(array, group, lambda copy: copy.wait_send())
        pair_copy(group).wait_send()
        for array in (DY, XF):
            for other in range(2):
                dup_copy(array, group, other).wait_send()
        return carry

    lax.fori_loop(0, GROUPS, first_sent, 0)

    finish_forward(0)
    finish_forward(1)
    for copy in gain_copies:
        copy.wait_recv()
    total = gain_ring[0]
    for index in range(1, 8):
        total = total + gain_ring[index]
    gain_sum[1] = total
    twin_copy = remote(gain_sum.at[1], gain_near.at[0], S_GAIN + 8, twin)
    twin_copy.start()
    finish_forward(2)
    twin_copy.wait_recv()
    gain_sum[2] = gain_sum[1] + gain_near[0]
    pair_sum = remote(gain_sum.at[2], gain_near.at[1], S_GAIN + 9, pair)
    pair_sum.start()
    finish_forward(3)

    stores = []

    def collect(which, hbm):
        for slot in others:
            back_copy(which, slot, offset_of(slot)).wait_recv()
        rows = dot(picked[which], back[which].reshape(SLOTS * ROWS, HALF))
        outs[which] = rows.astype(BF16)
        for half in range(2):
            store = pltpu.make_async_copy(
                outs.at[which, pl.ds(half * TOK, TOK)],
                hbm.at[0, :, pl.ds(half * HALF, HALF)],
                local_sem.at[9 + which * 2 + half],
            )
            store.start()
            stores.append(store)

    collect(BWD, ob_hbm)
    collect(FWD, of_hbm)
    pair_sum.wait_recv()
    total = gain_sum[2] + gain_near[1]
    for r in range(28):
        og_ref[:, r * 128 : (r + 1) * 128] = total[r : r + 1, :]

    for copy in gain_copies + [twin_copy, pair_sum]:
        copy.wait_send()

    def last_sent(group, carry):
        for which in (BWD, FWD):
            each_back(which, group, lambda copy: copy.wait_send())
            part_copy(which, group).wait_send()
        return carry

    lax.fori_loop(0, GROUPS, last_sent, 0)
    for store in stores:
        store.wait()


def chunks(*lead):
    return pltpu.VMEM((*lead, SLOTS, ROWS, HALF), BF16)


def body(
    fwd_prev,
    bwd_next,
    bwd_input,
    norm_gain,
    w_gate,
    w_up,
    w_down,
    fwd_routes,
    fwd_gates,
    bwd_routes,
    bwd_gates,
):
    lines = [v.reshape(1, TOK) for v in (fwd_routes, fwd_gates, bwd_routes, bwd_gates)]
    vmem = pl.BlockSpec(memory_space=pltpu.VMEM)
    anywhere = pl.BlockSpec(memory_space=pl.ANY)
    fwd_out, bwd_grad, gain_grad = pl.pallas_call(
        kernel,
        out_shape=(
            jax.ShapeDtypeStruct(fwd_prev.shape, BF16),
            jax.ShapeDtypeStruct(fwd_prev.shape, BF16),
            jax.ShapeDtypeStruct((1, D), F32),
        ),
        in_specs=[vmem] * 5 + [anywhere] * 6,
        out_specs=(anywhere, anywhere, vmem),
        scratch_shapes=[
            pltpu.VMEM((3, 2 * TOK, HALF), BF16),
            chunks(3),
            chunks(3),
            chunks(),
            chunks(2),
            chunks(2),
            chunks(2),
            chunks(2),
            pltpu.VMEM((2, GROUPS, ROWS, D), F32),
            chunks(2),
            chunks(2),
            pltpu.VMEM((2, 2 * TOK, HALF), BF16),
            pltpu.VMEM((2, D, SLICE), BF16),
            pltpu.VMEM((2, D, SLICE), BF16),
            pltpu.VMEM((2, SLICE, D), BF16),
            pltpu.VMEM((2 * ROWS, D), BF16),
            pltpu.VMEM((2 * ROWS, D), BF16),
            pltpu.VMEM((2 * ROWS, D), F32),
            pltpu.VMEM((8, TOK), F32),
            pltpu.VMEM((SLOTS, 8, TOK), F32),
            pltpu.VMEM((2, 8, TOK), F32),
            pltpu.VMEM((1, D), F32),
            pltpu.VMEM((8, 32, 128), F32),
            pltpu.VMEM((3, 32, 128), F32),
            pltpu.VMEM((2, 32, 128), F32),
            pltpu.VMEM((2, 2 * TOK, SLOTS * ROWS), BF16),
            pltpu.SemaphoreType.DMA((N_SEM,)),
            pltpu.SemaphoreType.DMA((N_SEM,)),
            pltpu.SemaphoreType.DMA((13,)),
        ],
        compiler_params=pltpu.CompilerParams(
            collective_id=0, has_side_effects=True, vmem_limit_bytes=62 * 2**20
        ),
    )(*lines, norm_gain, fwd_prev, bwd_next, bwd_input, w_gate, w_up, w_down)
    return (fwd_out, bwd_grad, gain_grad)


def solution(mesh):
    rows = P("pipe", "expert", None)
    columns = P("pipe", None, "expert")
    placed = (rows, rows, rows, P("pipe", None), columns, columns, rows, rows, rows, rows, rows)
    return jax.shard_map(
        body,
        mesh=mesh,
        in_specs=placed,
        out_specs=(rows, rows, P("pipe", None)),
        check_vma=False,
    )
```

```python
import jax
import jax.numpy as jnp
from jax import lax
from jax.experimental import pallas as pl
from jax.experimental.pallas import tpu as pltpu
from jax.sharding import PartitionSpec as P

MESH = pl.DeviceIdType.MESH
F32 = jnp.float32
BF16 = jnp.bfloat16

EPS = 1e-06
D = 3584
HALF = D // 2
TOK = 128
CAP = 24
ROWS = 2 * CAP
SLICE = 256
AHEAD = 2
STAY = 2
SLOTS = 8
GROUPS = SLOTS // 2
PIPE = 8

XB, DY, XF = 0, 1, 2
BWD, FWD = 0, 1

S_META = 0
S_WEIGHT = 9
S_RING = 12
S_PAIR = 36
S_DUP = 40
S_PART = 98
S_BACK = 64
S_GAIN = 80
S_META_RING = 90
N_SEM = 114


def dot(left, right):
    return jnp.dot(left, right, preferred_element_type=F32)


def contract_last(left, right):
    return lax.dot_general(left, right, (((1,), (1,)), ((), ())), preferred_element_type=F32)


def iota(shape, dim):
    return lax.broadcasted_iota(jnp.int32, shape, dim).astype(F32)


def halves(chunk):
    values = chunk.astype(F32)
    return values[:CAP], values[CAP:]


def inverse_rms(left, right):
    total = jnp.sum(left * left, axis=-1, keepdims=True)
    total = total + jnp.sum(right * right, axis=-1, keepdims=True)
    return lax.rsqrt(total * (1.0 / D) + EPS)


def earlier():
    return (iota((TOK, TOK), 0) < iota((TOK, TOK), 1)).astype(BF16)


def places(routes, z):
    onehot = (iota((8, TOK), 0) == routes).astype(F32)
    before = dot(onehot.astype(BF16), earlier())
    position = jnp.sum(onehot * before, axis=0, keepdims=True)
    ahead = routes - z.astype(F32)
    ahead = jnp.where(ahead < 0, ahead + 8, ahead)
    near = jnp.minimum(ahead, 8 - ahead)
    group = jnp.where(near == 2, 0.0, jnp.where(near == 3, 2.0, jnp.where(near == 1, 3.0, 1.0)))
    slot = 2 * group + jnp.where(ahead >= 4, 1.0, 0.0)
    return slot * ROWS + position


def offsets(group):
    first = (2 + 3 * group) % 5
    return first, 4 * ((4 - first) // 4) - first


def kernel(
    routes_f,
    gates_f,
    routes_b,
    gates_b,
    gain,
    x_hbm,
    dy_hbm,
    xb_hbm,
    wg_hbm,
    wu_hbm,
    wd_hbm,
    of_hbm,
    ob_hbm,
    og_ref,
    raw,
    sent,
    landed,
    pair_xb,
    all_dy,
    all_x,
    part_out,
    part_in,
    own_part,
    final,
    back,
    outs,
    wg,
    wu,
    wd,
    normed,
    grads,
    acc,
    meta,
    ring_meta,
    near_meta,
    gain_acc,
    gain_ring,
    gain_sum,
    gain_near,
    gate_cols,
    picked_first,
    picked_last,
    send_sem,
    recv_sem,
    local_sem,
):
    pipe = lax.axis_index("pipe")
    place = lax.axis_index("expert")
    z = place // 4
    xh = (place // 2) % 2
    core = place % 2
    odd = pipe % 2
    even = 1 - odd

    def at_ring(offset, ahead=0):
        return {
            "pipe": lax.rem(pipe + ahead + PIPE, PIPE),
            "expert": lax.rem(z + offset + 8, 8) * 4 + xh * 2 + core,
        }

    pair = {"pipe": pipe, "expert": z * 4 + (1 - xh) * 2 + core}
    twin = {"pipe": pipe, "expert": z * 4 + xh * 2 + (1 - core)}

    def at_section(distance):
        return {"pipe": lax.rem(pipe + distance + PIPE, PIPE), "expert": place}

    def beside(other):
        side = (1 - xh) if other else xh
        return {"pipe": pipe + 1 - 2 * odd, "expert": z * 4 + side * 2 + core}

    def remote(src, dst, sem, device):
        return pltpu.make_async_remote_copy(
            src_ref=src,
            dst_ref=dst,
            send_sem=send_sem.at[sem],
            recv_sem=recv_sem.at[sem],
            device_id=device,
            device_id_type=MESH,
        )

    loads = []
    for array, hbm in ((XB, xb_hbm), (DY, dy_hbm), (XF, x_hbm)):
        for half in range(2):
            loads.append(
                pltpu.make_async_copy(
                    hbm.at[0, :, pl.ds(half * HALF, HALF)],
                    raw.at[array, pl.ds(half * TOK, TOK)],
                    local_sem.at[array * 2 + half],
                )
            )
    for index, (hbm, vmem) in enumerate(((wg_hbm, wg), (wu_hbm, wu), (wd_hbm, wd))):
        loads.append(pltpu.make_async_copy(hbm.at[0], vmem.at[0], local_sem.at[6 + index]))
    for load in loads:
        load.start()

    barrier = pltpu.get_barrier_semaphore()
    partners = [at_ring(k) for k in range(1, 8)] + [pair, twin]
    partners += [beside(0), beside(1), at_section(2 * odd - 1)]
    partners += [at_ring(k, ahead) for ahead in (-2, 2) for k in range(8)]
    for device in partners:
        pl.semaphore_signal(barrier, inc=1, device_id=device, device_id_type=MESH)

    meta[...] = jnp.zeros_like(meta)
    for line, ref in enumerate((routes_f, gates_f, routes_b, gates_b)):
        meta[line : line + 1, :] = ref[...].astype(F32)

    def offset_of(slot):
        return offsets(slot // 2)[slot % 2]

    others = [slot for slot in range(SLOTS) if offset_of(slot)]

    metas = [
        remote(meta, near_meta.at[0], S_META, at_section(-1)),
        remote(meta, near_meta.at[1], S_META + 1, at_section(1)),
    ]
    for slot in others:
        metas.append(
            remote(meta, ring_meta.at[slot], S_META_RING + slot, at_ring(offset_of(slot)))
        )
    weights = [
        remote(hbm.at[0], vmem.at[1], S_WEIGHT + index, twin)
        for index, (hbm, vmem) in enumerate(((wg_hbm, wg), (wu_hbm, wu), (wd_hbm, wd)))
    ]

    ahead_of = (0, -2 * even, 2 * odd)

    def ring_copy(array, slot, offset):
        return remote(
            sent.at[array, slot],
            landed.at[array, slot],
            S_RING + array * 8 + slot,
            at_ring(offset, ahead_of[array]),
        )

    def each_ring(array, group, act, stay=lambda: None):
        one, two = offsets(group)
        act(ring_copy(array, 2 * group + 1, two))
        moved = (0, even, odd)[array]
        goes = (one != 0) if array == XB else (one != 0) | (moved == 1)

        @pl.when(goes)
        def _():
            act(ring_copy(array, 2 * group, one))

        @pl.when(jnp.logical_not(goes))
        def _():
            stay()

    def prepare(array, routes):
        base = places(routes, z)

        def step(group, carry):
            row = iota((2 * ROWS, TOK), 0) + (group * (2 * ROWS)).astype(F32)
            picks = jnp.concatenate([row == base, row == base + CAP], axis=1)
            picks = picks.astype(F32).astype(BF16)
            rows = dot(picks, raw[array]).astype(BF16)
            sent[array, pl.ds(2 * group, 2)] = rows.reshape(2, ROWS, HALF)
            return carry

        lax.fori_loop(0, GROUPS, step, 0)

    def send_group(array, group):
        def keep():
            landed[array, STAY] = sent[array, STAY]

        each_ring(array, group, lambda copy: copy.start(), keep)

    def wait_landed(array, group):
        each_ring(array, group, lambda copy: copy.wait_recv())

    loads[0].wait()
    loads[1].wait()
    prepare(XB, meta[2:3, :])
    pl.semaphore_wait(barrier, len(partners))
    for group in (3, 0, 1, 2):
        send_group(XB, group)
    for copy in metas + weights:
        copy.start()
    ring_meta[STAY] = meta[...]
    metas[1].wait_recv()
    loads[2].wait()
    loads[3].wait()
    prepare(DY, near_meta[1, 2:3, :])

    def pair_copy(group):
        two = pl.ds(2 * group, 2)
        return remote(landed.at[XB, two], pair_xb.at[two], S_PAIR + group, pair)

    def dup_copy(array, group, other):
        two = pl.ds(2 * group, 2)
        dst = all_dy if array == DY else all_x
        sem = S_DUP + (array - 1) * 8 + other * 4 + group
        return remote(landed.at[array, two], dst.at[other, two], sem, beside(other))

    def relay_pair(group):
        wait_landed(XB, group)
        pair_copy(group).start()

    def relay_dup(array, group):
        wait_landed(array, group)
        dup_copy(array, group, 0).start()
        dup_copy(array, group, 1).start()

    def prepare_collect(which, routes):
        base = jnp.broadcast_to(places(routes, z), (TOK, TOK)).T[:, 0:1]
        for first, ref in ((0, picked_first), (6, picked_last)):
            column = iota((TOK, ref.shape[-1]), 1) + first * ROWS
            picks = jnp.concatenate([column == base, column == base + CAP], axis=0)
            ref[which] = picks.astype(F32).astype(BF16)

    relay_pair(3)
    relay_pair(0)
    send_group(DY, 0)
    send_group(DY, 1)
    send_group(DY, 2)
    send_group(DY, 3)
    metas[0].wait_recv()
    loads[4].wait()
    loads[5].wait()
    prepare(XF, near_meta[0, 0:1, :])
    relay_pair(1)
    relay_pair(2)
    relay_dup(DY, 0)
    relay_dup(DY, 1)
    send_group(XF, 0)
    send_group(XF, 1)
    send_group(XF, 2)
    send_group(XF, 3)
    relay_dup(DY, 2)
    relay_dup(DY, 3)

    def prepare_gates(which):
        line = 2 * (1 - which)
        routes = ring_meta[:, line, :]
        gates = ring_meta[:, line + 1, :]
        mine = (routes == z.astype(F32)).astype(F32)
        before = dot(mine.astype(BF16), earlier())
        chosen = jnp.where(mine > 0, before, -1.0)
        for slot in range(SLOTS):
            one = slice(slot, slot + 1)
            found = jnp.where(iota((CAP, TOK), 0) == chosen[one], gates[one], 0.0)
            column = jnp.sum(found, axis=1, keepdims=True)
            gate_cols[which, slot] = jnp.broadcast_to(column, (CAP, TOK))

    for copy in metas[2:]:
        copy.wait_recv()
    prepare_gates(BWD)
    prepare_gates(FWD)
    prepare_collect(FWD, meta[0:1, :])
    prepare_collect(BWD, meta[2:3, :])

    gain_left = gain[:, :HALF]
    gain_right = gain[:, HALF:]

    def gather_rows(own, other, group, to, scaled):
        for side, ref in enumerate((own, other)):
            lefts, rights = [], []
            for s in range(2):
                left, right = halves(ref(2 * group + s))
                if scaled:
                    inverse = inverse_rms(left, right)
                    left = left * inverse * gain_left
                    right = right * inverse * gain_right
                lefts.append(left)
                rights.append(right)
            rows = pl.ds(side * ROWS, ROWS)
            to[rows, pl.ds(0, HALF)] = jnp.concatenate(lefts, axis=0).astype(BF16)
            to[rows, pl.ds(HALF, HALF)] = jnp.concatenate(rights, axis=0).astype(BF16)

    def part_copy(which, slot):
        return remote(
            part_out.at[which, slot], part_in.at[which, slot], S_PART + which * 8 + slot, pair
        )

    def share(which, group, start):
        for s in range(2):
            rows = pl.ds(ROWS + s * CAP, CAP)
            chunk = jnp.concatenate([acc[rows, pl.ds(0, HALF)], acc[rows, pl.ds(HALF, HALF)]], axis=0)
            part_out[which, 2 * group + s] = chunk.astype(BF16)
            if start is True:
                part_copy(which, 2 * group + s).start()
        if start is not True:

            @pl.when(start)
            def _():
                part_copy(which, 2 * group).start()
                part_copy(which, 2 * group + 1).start()

        own_part[which, group] = acc[pl.ds(0, ROWS), :]

    for load in loads[6:]:
        load.wait()
    for copy in weights:
        copy.wait_recv()

    def back_copy(which, slot, offset):
        return remote(
            final.at[which, slot],
            back.at[which, slot],
            S_BACK + which * 8 + slot,
            at_ring(-offset),
        )

    def each_back(which, group, s, act, stay=lambda: None):
        one, two = offsets(group)
        if s == 1:
            act(back_copy(which, 2 * group + 1, two))
            return

        @pl.when(one != 0)
        def _():
            act(back_copy(which, 2 * group, one))

        @pl.when(one == 0)
        def _():
            stay()

    def send_back(which, group, s):
        def keep():
            back[which, STAY] = final[which, STAY]

        each_back(which, group, s, lambda copy: copy.start(), keep)

    def summed(which, group, s):
        rows = pl.ds(s * CAP, CAP)
        left, right = halves(part_in[which, 2 * group + s])
        gate = gate_cols[which, 2 * group + s, :, 0:1]
        left = gate * (left + own_part[which, group, rows, pl.ds(0, HALF)])
        right = gate * (right + own_part[which, group, rows, pl.ds(HALF, HALF)])
        return left, right

    def finish_forward(slot):
        part_copy(FWD, slot).wait_recv()
        if slot + AHEAD < SLOTS:
            part_copy(FWD, slot + AHEAD).start()
        q_left, q_right = summed(FWD, slot // 2, slot % 2)
        x_left, x_right = halves(all_x[0, slot])
        chunk = jnp.concatenate([x_left + q_left, x_right + q_right], axis=0)
        final[FWD, slot] = chunk.astype(BF16)
        send_back(FWD, slot // 2, slot % 2)

    gain_acc[...] = jnp.zeros_like(gain_acc)

    def finish_backward(group):
        for s in range(2):
            slot = 2 * group + s
            part_copy(BWD, slot).wait_recv()
            dn_left, dn_right = summed(BWD, group, s)
            x_left, x_right = halves(landed[XB, slot])
            inverse = inverse_rms(x_left, x_right)
            u_left = dn_left * gain_left
            u_right = dn_right * gain_right
            inner = jnp.sum(u_left * x_left, axis=-1, keepdims=True)
            inner = inner + jnp.sum(u_right * x_right, axis=-1, keepdims=True)
            scale = inverse * inverse * inverse * (inner * (1.0 / D))
            dy_left, dy_right = halves(all_dy[0, slot])
            g_left = dy_left + inverse * u_left - x_left * scale
            g_right = dy_right + inverse * u_right - x_right * scale
            final[BWD, slot] = jnp.concatenate([g_left, g_right], axis=0).astype(BF16)
            send_back(BWD, group, s)
            gain_acc[:, pl.ds(0, HALF)] += jnp.sum(
                dn_left * x_left * inverse, axis=0, keepdims=True
            )
            gain_acc[:, pl.ds(HALF, HALF)] += jnp.sum(
                dn_right * x_right * inverse, axis=0, keepdims=True
            )

    def backward(group, carry):
        pair_copy(group).wait_recv()
        dup_copy(DY, group, 0).wait_recv()
        dup_copy(DY, group, 1).wait_recv()
        gather_rows(
            lambda j: landed[XB, j], lambda j: pair_xb[j], group, normed, True
        )
        gather_rows(lambda j: all_dy[0, j], lambda j: all_dy[1, j], group, grads, False)
        acc[...] = jnp.zeros_like(acc)

        def hidden(h, inner):
            rows = normed[...]
            a = dot(rows, wg[h])
            b = dot(rows, wu[h])
            dh = contract_last(grads[...], wd[h])
            sig = 1.0 / (1.0 + jnp.exp(-a))
            da = (dh * b * sig * (1.0 + a * (1.0 - sig))).astype(BF16)
            db = (dh * a * sig).astype(BF16)
            acc[...] += contract_last(da, wg[h]) + contract_last(db, wu[h])
            return inner

        lax.fori_loop(0, 2, hidden, 0)
        share(BWD, group, True)
        relay_dup(XF, group)

        return carry

    lax.fori_loop(0, GROUPS, backward, 0)

    def forward(group, carry):
        dup_copy(XF, group, 0).wait_recv()
        dup_copy(XF, group, 1).wait_recv()
        gather_rows(lambda j: all_x[0, j], lambda j: all_x[1, j], group, normed, True)
        acc[...] = jnp.zeros_like(acc)

        def hidden(h, inner):
            rows = normed[...]
            a = dot(rows, wg[h])
            b = dot(rows, wu[h])
            act = (a / (1.0 + jnp.exp(-a)) * b).astype(BF16)
            acc[...] += dot(act, wd[h])
            return inner

        lax.fori_loop(0, 2, hidden, 0)
        share(FWD, group, group == 0)
        finish_backward(group)
        return carry

    lax.fori_loop(0, GROUPS, forward, 0)


    gain_sum[0] = jnp.zeros((32, 128), F32)
    for r in range(28):
        gain_sum[0, r : r + 1, :] = gain_acc[:, r * 128 : (r + 1) * 128]
    gain_ring[z] = gain_sum[0]
    gain_copies = [
        remote(gain_sum.at[0], gain_ring.at[z], S_GAIN + slot, at_ring(offset_of(slot)))
        for slot in others
    ]
    for copy in gain_copies:
        copy.start()

    for copy in metas + weights:
        copy.wait_send()

    def first_sent(group, carry):
        for array in (XB, DY, XF):
            each_ring(array, group, lambda copy: copy.wait_send())
        pair_copy(group).wait_send()
        for array in (DY, XF):
            for other in range(2):
                dup_copy(array, group, other).wait_send()
        return carry

    lax.fori_loop(0, GROUPS, first_sent, 0)

    for slot in range(2, AHEAD):
        part_copy(FWD, slot).start()
    for slot in range(4):
        finish_forward(slot)
    for copy in gain_copies:
        copy.wait_recv()
    total = gain_ring[0]
    for index in range(1, 8):
        total = total + gain_ring[index]
    gain_sum[1] = total
    twin_copy = remote(gain_sum.at[1], gain_near.at[0], S_GAIN + 8, twin)
    twin_copy.start()
    finish_forward(4)
    finish_forward(5)
    twin_copy.wait_recv()
    gain_sum[2] = gain_sum[1] + gain_near[0]
    pair_sum = remote(gain_sum.at[2], gain_near.at[1], S_GAIN + 9, pair)
    pair_sum.start()
    finish_forward(6)
    finish_forward(7)

    stores = []

    def collect(which, hbm):
        for slot in others[:-2]:
            back_copy(which, slot, offset_of(slot)).wait_recv()
        acc_rows = dot(picked_first[which], back[which, 0:6].reshape(6 * ROWS, HALF))
        for slot in others[-2:]:
            back_copy(which, slot, offset_of(slot)).wait_recv()
        rows = acc_rows + dot(picked_last[which], back[which, 6:8].reshape(2 * ROWS, HALF))
        outs[which] = rows.astype(BF16)
        for half in range(2):
            store = pltpu.make_async_copy(
                outs.at[which, pl.ds(half * TOK, TOK)],
                hbm.at[0, :, pl.ds(half * HALF, HALF)],
                local_sem.at[9 + which * 2 + half],
            )
            store.start()
            stores.append(store)

    collect(BWD, ob_hbm)
    collect(FWD, of_hbm)
    pair_sum.wait_recv()
    total = gain_sum[2] + gain_near[1]
    for r in range(28):
        og_ref[:, r * 128 : (r + 1) * 128] = total[r : r + 1, :]

    for copy in gain_copies + [twin_copy, pair_sum]:
        copy.wait_send()

    def last_sent(group, carry):
        for which in (BWD, FWD):
            for s in range(2):
                each_back(which, group, s, lambda copy: copy.wait_send())
                part_copy(which, 2 * group + s).wait_send()
        return carry

    lax.fori_loop(0, GROUPS, last_sent, 0)
    for store in stores:
        store.wait()


def chunks(*lead):
    return pltpu.VMEM((*lead, SLOTS, ROWS, HALF), BF16)


def body(
    fwd_prev,
    bwd_next,
    bwd_input,
    norm_gain,
    w_gate,
    w_up,
    w_down,
    fwd_routes,
    fwd_gates,
    bwd_routes,
    bwd_gates,
):
    lines = [v.reshape(1, TOK) for v in (fwd_routes, fwd_gates, bwd_routes, bwd_gates)]
    vmem = pl.BlockSpec(memory_space=pltpu.VMEM)
    anywhere = pl.BlockSpec(memory_space=pl.ANY)
    fwd_out, bwd_grad, gain_grad = pl.pallas_call(
        kernel,
        out_shape=(
            jax.ShapeDtypeStruct(fwd_prev.shape, BF16),
            jax.ShapeDtypeStruct(fwd_prev.shape, BF16),
            jax.ShapeDtypeStruct((1, D), F32),
        ),
        in_specs=[vmem] * 5 + [anywhere] * 6,
        out_specs=(anywhere, anywhere, vmem),
        scratch_shapes=[
            pltpu.VMEM((3, 2 * TOK, HALF), BF16),
            chunks(3),
            chunks(3),
            chunks(),
            chunks(2),
            chunks(2),
            chunks(2),
            chunks(2),
            pltpu.VMEM((2, GROUPS, ROWS, D), F32),
            chunks(2),
            chunks(2),
            pltpu.VMEM((2, 2 * TOK, HALF), BF16),
            pltpu.VMEM((2, D, SLICE), BF16),
            pltpu.VMEM((2, D, SLICE), BF16),
            pltpu.VMEM((2, SLICE, D), BF16),
            pltpu.VMEM((2 * ROWS, D), BF16),
            pltpu.VMEM((2 * ROWS, D), BF16),
            pltpu.VMEM((2 * ROWS, D), F32),
            pltpu.VMEM((8, TOK), F32),
            pltpu.VMEM((SLOTS, 8, TOK), F32),
            pltpu.VMEM((2, 8, TOK), F32),
            pltpu.VMEM((1, D), F32),
            pltpu.VMEM((8, 32, 128), F32),
            pltpu.VMEM((3, 32, 128), F32),
            pltpu.VMEM((2, 32, 128), F32),
            pltpu.VMEM((2, SLOTS, CAP, TOK), F32),
            pltpu.VMEM((2, 2 * TOK, 6 * ROWS), BF16),
            pltpu.VMEM((2, 2 * TOK, 2 * ROWS), BF16),
            pltpu.SemaphoreType.DMA((N_SEM,)),
            pltpu.SemaphoreType.DMA((N_SEM,)),
            pltpu.SemaphoreType.DMA((13,)),
        ],
        compiler_params=pltpu.CompilerParams(
            collective_id=0, has_side_effects=True, vmem_limit_bytes=62 * 2**20
        ),
    )(*lines, norm_gain, fwd_prev, bwd_next, bwd_input, w_gate, w_up, w_down)
    return (fwd_out, bwd_grad, gain_grad)


def solution(mesh):
    rows = P("pipe", "expert", None)
    columns = P("pipe", None, "expert")
    placed = (rows, rows, rows, P("pipe", None), columns, columns, rows, rows, rows, rows, rows)
    return jax.shard_map(
        body,
        mesh=mesh,
        in_specs=placed,
        out_specs=(rows, rows, P("pipe", None)),
        check_vma=False,
    )
```
